32 devices in a mesh: grp: 2 (over x), seq: 16 (over z, y, core).
Axes of the slice: x: 2, y: 2, z: 4, core: 2. Of those that a mesh axis runs over, the one named last changes fastest.
Arguments:
- layer_ids: int32 [2], P('grp'), parts along dimension 0, may hold values from 0 to 15
- seq_ids: int32 [128], P(('grp', 'seq')), parts along dimension 0, may hold values from 0 to 1
- out_eigen: float32 [16, 32768], P(None, 'seq'), as said below
- in_eigen: float32 [16, 8192], P(None, 'seq'), as said below
- query_out: float32 [1, 4, 32, 32768], P(None, 'grp', None, 'seq'), parts along dimension 1, may hold values from -6 to 6
- query_in: float32 [1, 4, 32, 8192], P(None, 'grp', None, 'seq'), parts along dimension 1, may hold values from -6 to 6
- train_out: float32 [1, 64, 32, 32768], P(None, ('grp', 'seq')), parts along dimension 1, may hold values from -2.4 to 2.4
- train_in: float32 [1, 64, 32, 8192], P(None, ('grp', 'seq')), parts along dimension 1, may hold values from -2.4 to 2.4
Outputs:
- influence: float32 [4, 64], P('grp', 'seq'), parts along dimension 0
The draws below stay inside these ranges and needn't reach their ends.
There are 2 independent parts, one for each index of `grp`. The reference program is written for one: setup_inputs(seed, part) draws one part's arguments, and reference() takes and returns one part's arrays. A program takes and returns all parts, laid end to end along the dimension named above; an argument that names none is the same for every part. Nothing has to cross between parts.
Inputs may be any that keep to these rules, and one draw needn't show every extreme that they name: `out_eigen`: every entry is positive. `in_eigen`: every entry is positive.
All inputs are finite; a program needn't handle non-finite values.
Results may differ from the reference program's by a relative error of at most 0.00015.
Values sent between devices are 32-bit elements; how exact they have to be, the bound alone decides.
A program may use at most 64 MiB of HBM per device.

```python
import jax
import jax.numpy as jnp
from jax import lax

WIDTH = 8192
OUT_WIDTH = 32768
RANK = 32
LAYERS = 16
SAMPLED = 1
QUERIES = 2
POOL_DEV = 2
SEL_DEV = 4
TRAIN_POOL = 32
TRAIN = 64


def spectrum_draw(key, row_count, col_count):
    position = jnp.arange(col_count, dtype=jnp.float32) / col_count
    falloff = 10.0 ** (-position)
    roughness = jnp.exp(jax.random.uniform(key, (row_count, col_count), jnp.float32, jnp.log(0.5), jnp.log(1.5)))
    layer_scale = jnp.exp(jax.random.uniform(jax.random.fold_in(key, 7), (row_count, 1), jnp.float32, jnp.log(0.5), jnp.log(2.0)))
    return falloff[None, :] * roughness * layer_scale


def draw_out_eigen(key, part):
    key = jax.random.fold_in(key, 11)
    return spectrum_draw(key, LAYERS, OUT_WIDTH)


def draw_in_eigen(key, part):
    key = jax.random.fold_in(key, 23)
    return spectrum_draw(key, LAYERS, WIDTH)


def with_ends(result, stream_key, smallest, high):
    dims = result.shape
    index_at = [jax.random.randint(jax.random.fold_in(stream_key, axis), (), 0, dims[axis]) for axis in range(len(dims))]
    result = result.at[tuple(index_at)].set(smallest)
    longest = dims.index(max(dims))
    index_at[longest] = (index_at[longest] + 1) % dims[longest]
    return result.at[tuple(index_at)].set(high)


def shard_levels(stream_key, dims, shards, smallest, top_value):
    level = 1.0
    for dim, shards_of in shards:
        heights = jax.random.uniform(jax.random.fold_in(jax.random.fold_in(stream_key, 6), dim), (shards_of,), jnp.float32, smallest / len(shards), top_value / len(shards))
        level = level * jnp.repeat(jnp.exp(heights), dims[dim] // shards_of).reshape((-1,) + (1,) * (len(dims) - 1 - dim))
    return level


def bell_draw(rng, dims, spread, limit, cuts=(), kind=jnp.bfloat16):
    values = jax.random.normal(rng, dims, jnp.float32) * spread
    if len(cuts) > 0:
        values = shard_levels(rng, dims, cuts, -0.22, 0.18) * values
    return jnp.clip(values, min=-limit, max=limit).astype(kind)


def setup_inputs(seed: int = 0, part: int = 0) -> dict:
    key_list = jax.random.split(jax.random.key(seed), 9)
    own_keys = jax.random.split(jax.random.fold_in(key_list[8], part), 9)
    return {
        "layer_ids": jax.random.randint(own_keys[0], (SAMPLED,), 0, LAYERS).astype(jnp.int32),
        "seq_ids": with_ends(jax.random.randint(own_keys[1], (TRAIN,), 0, POOL_DEV), jax.random.fold_in(own_keys[1], 1), 0, POOL_DEV - 1).astype(jnp.int32),
        "out_eigen": draw_out_eigen(jax.random.fold_in(key_list[8], 71), part),
        "in_eigen": draw_in_eigen(jax.random.fold_in(key_list[8], 71), part),
        "query_out": bell_draw(own_keys[4], (SAMPLED, QUERIES, RANK, OUT_WIDTH), 1.0, 6.0, ((3, 16),), jnp.float32),
        "query_in": bell_draw(own_keys[5], (SAMPLED, QUERIES, RANK, WIDTH), 1.0, 6.0, ((3, 16),), jnp.float32),
        "train_out": bell_draw(own_keys[6], (SAMPLED, TRAIN_POOL, RANK, OUT_WIDTH), 0.4, 2.4, ((1, 16),), jnp.float32),
        "train_in": bell_draw(own_keys[7], (SAMPLED, TRAIN_POOL, RANK, WIDTH), 0.4, 2.4, ((1, 16),), jnp.float32),
    }


damping = 0.1
epsilon = 1e-06

def precondition(factors, stored_values, layer_ids):
    chosen = stored_values[layer_ids]
    return factors / (chosen[:, None, None, :] + damping)

def reference(layer_ids, seq_ids, out_eigen, in_eigen, query_out, query_in, train_out, train_in):
    scaled_out = precondition(query_out, out_eigen, layer_ids)
    scaled_in = precondition(query_in, in_eigen, layer_ids)
    gram_out = jnp.einsum('lqri,lqsi->lqrs', scaled_out, scaled_out, precision=lax.Precision.HIGHEST)
    gram_in = jnp.einsum('lqri,lqsi->lqrs', scaled_in, scaled_in, precision=lax.Precision.HIGHEST)
    query_norm = lax.optimization_barrier(jnp.sum(gram_out * gram_in, axis=(0, 2, 3)))

    def one_layer(layer_items):
        left_out, left_in, right_out, right_in = layer_items
        cross_out = jnp.einsum('qri,tsi->qrts', left_out, right_out, precision=lax.Precision.HIGHEST)
        cross_in = jnp.einsum('qri,tsi->qrts', left_in, right_in, precision=lax.Precision.HIGHEST)
        return lax.optimization_barrier(jnp.sum(cross_out * cross_in, axis=(1, 3)))
    unscaled = lax.optimization_barrier(jnp.sum(lax.map(one_layer, (scaled_out, scaled_in, train_out, train_in)), axis=0))
    column = jnp.arange(TRAIN, dtype=jnp.int32) // SEL_DEV * POOL_DEV + seq_ids.astype(jnp.int32)
    picked = jnp.take(unscaled, column, axis=1)
    return picked / jnp.sqrt(query_norm + epsilon)[:, None]
```

```python
import functools

import jax
import jax.numpy as jnp
from jax import lax
from jax.experimental import pallas as pl
from jax.experimental.pallas import tpu as pltpu
from jax.sharding import PartitionSpec as P

damping = 0.1
epsilon = 1e-06

MESH = pl.DeviceIdType.MESH
CORES = 2
PLANE_CHIPS = 4
UP, DOWN, SIDE_UP, SIDE_DOWN = range(4)


def split(x):
    high = x.astype(jnp.bfloat16)
    low = (x - high.astype(jnp.float32)).astype(jnp.bfloat16)
    return jnp.concatenate([high, low], axis=0)


def both(*conditions):
    return functools.reduce(jnp.logical_and, conditions)


def kernel(depth, rows_y, layer_ref, seq_ids_ref, out_eigen_ref, in_eigen_ref, query_out_ref, query_in_ref,
           train_out_ref, train_in_ref, result_ref,
           held, train, total, load_sem, recv_sem, send_sem, core_sem, extra_sem):
    shards, chunks, vectors, width = held.shape
    queries = result_ref.shape[0]
    rank = vectors // queries
    train_rows, out_all = train_out_ref.shape
    out_chunks = chunks - 1
    grp = lax.axis_index("grp")
    me = lax.axis_index("seq")
    core = lax.rem(me, CORES)
    y = lax.rem(me // CORES, rows_y)
    z = me // (CORES * rows_y)
    balanced = rows_y == 2 and depth >= 4
    last = depth - 1

    def index(at_z, at_y, at_core):
        return (at_z * rows_y + at_y) * CORES + at_core

    load_out = pltpu.make_async_copy(train_out_ref, train.at[:, pl.ds(0, out_all)], load_sem.at[0])
    load_in = pltpu.make_async_copy(train_in_ref, train.at[:, pl.ds(out_all, train_in_ref.shape[1])], load_sem.at[1])
    load_out.start()
    load_in.start()

    above, below = index(z + 1, y, core), index(z - 1, y, core)
    beside, sibling = index(z, 1 - y, core), index(z, y, 1 - core)
    has_above, has_below = z < last, z > 0

    barrier = pltpu.get_barrier_semaphore()

    def greet(other):
        pl.semaphore_signal(barrier, inc=1, device_id=(grp, other), device_id_type=MESH)

    greet(sibling)
    if rows_y == 2:
        greet(beside)
    pl.when(has_above)(lambda: greet(above))
    pl.when(has_below)(lambda: greet(below))

    def send(shard, chunk, other, sem):
        pltpu.make_async_remote_copy(
            src_ref=held.at[shard, chunk], dst_ref=held.at[shard, chunk],
            send_sem=sem, recv_sem=recv_sem.at[shard, chunk],
            device_id=(grp, other), device_id_type=MESH,
        ).start()

    def arrived(shard, chunk):
        pltpu.make_async_remote_copy(
            src_ref=held.at[shard, chunk], dst_ref=held.at[shard, chunk],
            send_sem=core_sem, recv_sem=recv_sem.at[shard, chunk],
            device_id=(grp, sibling), device_id_type=MESH,
        ).wait_recv()

    def sent(block, other, sem):
        pltpu.make_async_remote_copy(
            src_ref=block, dst_ref=block, send_sem=sem, recv_sem=recv_sem.at[0, 0],
            device_id=(grp, other), device_id_type=MESH,
        ).wait_send()

    layer = layer_ref[0]

    def damped(eigen_ref, query_ref, start):
        eigen = eigen_ref[:, start:start + width]
        stored = lax.broadcasted_iota(jnp.int32, eigen.shape, 0)
        chosen = jnp.sum(jnp.where(stored == layer, eigen, 0.0), axis=0, keepdims=True)
        return query_ref[:, start:start + width] / (chosen + damping)

    for chunk in range(out_chunks):
        held[me, chunk] = damped(out_eigen_ref, query_out_ref, chunk * width)
    held[me, out_chunks] = damped(in_eigen_ref, query_in_ref, 0)

    pl.semaphore_wait(barrier, rows_y + has_above.astype(jnp.int32) + has_below.astype(jnp.int32))

    for chunk in range(chunks):
        pl.when(has_above)(lambda: send(me, chunk, above, send_sem.at[UP, 0]))
        pl.when(has_below)(lambda: send(me, chunk, below, send_sem.at[DOWN, 0]))
        if rows_y == 2:
            send(me, chunk, beside, send_sem.at[SIDE_UP, 0])
        send(me, chunk, sibling, core_sem)

    total[...] = jnp.zeros_like(total)
    load_out.wait()
    load_in.wait()

    def absorb(shard, chunk):
        kind = chunk // out_chunks
        column = jnp.where(
            chunk < out_chunks, shard * (out_chunks * width) + chunk * width, out_all + shard * width)
        mine = split(held[shard, chunk])
        theirs = split(train[:, pl.ds(pl.multiple_of(column, width), width)])
        total[kind] += lax.dot_general(
            mine, jnp.concatenate([theirs, mine], axis=0), (((1,), (1,)), ((), ())),
            preferred_element_type=jnp.float32)

    def halved(chunk, at_core):
        return chunk < (chunks + 1) // 2 - at_core * (chunks % 2)

    def crosses(to_z, from_z, chunk, at_core):
        if not balanced:
            return True
        skip = jnp.logical_or(both(to_z == 1, from_z == 0), both(to_z == last - 1, from_z == last))
        half = jnp.logical_or(both(to_z == 0, from_z == 1), both(to_z == last, from_z == last - 1))
        return jnp.logical_not(jnp.logical_or(skip, both(half, halved(chunk, at_core))))

    def arrivals(step, chunk, at_core):
        up, down = z - step, z + step
        result = [
            (up >= 0, index(up, y, at_core), UP),
            (down <= last, index(down, y, at_core), DOWN),
        ]
        if rows_y == 2:
            up, down = z - (step - 1), z + (step - 1)
            result += [
                (both(up >= 0, crosses(z, up, chunk, at_core)), index(up, 1 - y, at_core), SIDE_UP),
                (both(step > 1, down <= last, crosses(z, down, chunk, at_core)),
                 index(down, 1 - y, at_core), SIDE_DOWN),
            ]
        if balanced:
            first = jnp.logical_or(both(z == 1, step == 2), both(z == last - 1, step == 2))
            final = both(jnp.logical_or(z == 0, z == last), step == depth, halved(chunk, at_core))
            end = jnp.where(z <= 1, 1 - z, last + last - 1 - z)
            result += [(jnp.logical_or(first, final), index(end, 1 - y, at_core), None)]
        return result

    def forward(step, chunk):
        for whether, shard, kind in arrivals(step, chunk, core):
            @pl.when(whether)
            def _():
                arrived(shard, chunk)
                if kind == UP:
                    pl.when(has_above)(lambda: send(shard, chunk, above, send_sem.at[UP, step]))
                    if rows_y == 2:
                        pl.when(crosses(z, z - step, chunk, core))(
                            lambda: send(shard, chunk, beside, send_sem.at[SIDE_UP, step]))
                if kind == DOWN:
                    pl.when(has_below)(lambda: send(shard, chunk, below, send_sem.at[DOWN, step]))
                    if rows_y == 2:
                        pl.when(crosses(z, z + step, chunk, core))(
                            lambda: send(shard, chunk, beside, send_sem.at[SIDE_DOWN, step]))
                if kind == SIDE_UP and balanced:
                    pl.when(both(step == 1, z == 0))(lambda: send(shard, chunk, above, extra_sem))
                    pl.when(both(step == 1, z == last))(lambda: send(shard, chunk, below, extra_sem))
                send(shard, chunk, sibling, core_sem)
        if balanced:
            opposite = index(z, 1 - y, core)
            late = both(step == last, halved(chunk, core))
            pl.when(both(late, z == 1))(lambda: send(opposite, chunk, below, extra_sem))
            pl.when(both(late, z == last - 1))(lambda: send(opposite, chunk, above, extra_sem))

    def absorb_all(step, chunk, at_core):
        for whether, shard, _ in arrivals(step, chunk, at_core):
            @pl.when(whether)
            def _():
                if at_core is not core:
                    arrived(shard, chunk)
                absorb(shard, chunk)

    def own(chunk, _):
        absorb(me, chunk)
        return 0

    def siblings(chunk, _):
        arrived(sibling, chunk)
        absorb(sibling, chunk)
        return 0

    lax.fori_loop(0, chunks, own, 0)

    steps = depth if rows_y == 2 else depth - 1
    other_core = 1 - core

    def tick(turn, _):
        step, chunk = turn // chunks + 1, lax.rem(turn, chunks)
        forward(step, chunk)
        absorb_all(step, chunk, core)

        @pl.when(step == 1)
        def _():
            siblings(chunk, 0)

        @pl.when(turn > 0)
        def _():
            before = turn - 1
            absorb_all(before // chunks + 1, lax.rem(before, chunks), other_core)
        return 0

    lax.fori_loop(0, steps * chunks, tick, 0)
    absorb_all(steps, chunks - 1, other_core)

    sent(held.at[pl.ds(0, shards // CORES)], sibling, core_sem)

    def left(step, _):
        pl.when(both(has_above, step <= z))(lambda: sent(held.at[0], above, send_sem.at[UP, step]))
        pl.when(both(has_below, step <= last - z))(lambda: sent(held.at[0], below, send_sem.at[DOWN, step]))
        if rows_y == 2:
            for kind, from_z, some in ((SIDE_UP, z - step, z >= step),
                                       (SIDE_DOWN, z + step, both(step > 0, z + step <= last))):
                def chunk_left(chunk, _):
                    return 0
                if not balanced:
                    pl.when(some)(lambda: sent(held.at[0], beside, send_sem.at[kind, step]))
                    continue
                skip = jnp.logical_or(both(z == 1, from_z == 0), both(z == last - 1, from_z == last))
                half = jnp.logical_or(both(z == 0, from_z == 1), both(z == last, from_z == last - 1))
                pl.when(both(some, jnp.logical_not(jnp.logical_or(skip, half))))(
                    lambda: sent(held.at[0], beside, send_sem.at[kind, step]))
                for at_core in range(CORES):
                    count = chunks // 2 + at_core * (chunks % 2)
                    pl.when(both(some, half, core == at_core))(
                        lambda: sent(held.at[0, pl.ds(0, count)], beside, send_sem.at[kind, step]))
        return 0

    lax.fori_loop(0, depth, left, 0)
    if balanced:
        for other, end, near in ((above, z == 0, z == last - 1), (below, z == last, z == 1)):
            pl.when(end)(lambda: sent(held.at[0], other, extra_sem))
            for at_core in range(CORES):
                count = (chunks + 1) // 2 - at_core * (chunks % 2)
                pl.when(both(near, core == at_core))(
                    lambda: sent(held.at[0, pl.ds(0, count)], other, extra_sem))

    def whole(kind):
        rows = total[kind, :vectors] + total[kind, vectors:]
        return (rows[:, :train_rows] + rows[:, train_rows:2 * train_rows],
                rows[:, 2 * train_rows:2 * train_rows + vectors] + rows[:, 2 * train_rows + vectors:])

    cross_out, gram_out = whole(0)
    cross_in, gram_in = whole(1)
    cross = cross_out * cross_in
    gram = gram_out * gram_in
    pool = train_rows // rank
    for query in range(queries):
        lines = slice(query * rank, (query + 1) * rank)
        norm = jnp.sum(gram[lines, lines], keepdims=True)
        scale = jnp.sqrt(norm + epsilon)
        picked = jnp.zeros(seq_ids_ref.shape, jnp.float32)
        for t in range(pool):
            unscaled = jnp.sum(cross[lines, t * rank:(t + 1) * rank], keepdims=True)
            picked += jnp.where(seq_ids_ref[...] == t, unscaled, 0.0)
        result_ref[query:query + 1, :] = picked / scale


def local(rows_y, layer_ids, seq_ids, out_eigen, in_eigen, query_out, query_in, train_out, train_in):
    shards = lax.axis_size("seq")
    _, queries, rank, out_cols = query_out.shape
    in_cols = query_in.shape[3]
    vectors = queries * rank
    train_rows = train_out.shape[1] * rank
    out_all, in_all = train_out.shape[3], train_in.shape[3]
    chunks = out_cols // in_cols + 1
    depth = shards // (CORES * rows_y)
    vmem = pl.BlockSpec(memory_space=pltpu.VMEM)
    smem = pl.BlockSpec(memory_space=pltpu.SMEM)
    anywhere = pl.BlockSpec(memory_space=pl.ANY)
    return pl.pallas_call(
        functools.partial(kernel, depth, rows_y),
        out_shape=jax.ShapeDtypeStruct((queries, seq_ids.shape[0]), jnp.float32),
        in_specs=[smem, vmem, vmem, vmem, vmem, vmem, anywhere, anywhere],
        out_specs=vmem,
        scratch_shapes=[
            pltpu.VMEM((shards, chunks, vectors, in_cols), jnp.float32),
            pltpu.VMEM((train_rows, out_all + in_all), jnp.float32),
            pltpu.VMEM((2, 2 * vectors, 2 * (train_rows + vectors)), jnp.float32),
            pltpu.SemaphoreType.DMA((2,)),
            pltpu.SemaphoreType.DMA((shards, chunks)),
            pltpu.SemaphoreType.DMA((4, depth)),
            pltpu.SemaphoreType.DMA,
            pltpu.SemaphoreType.DMA,
        ],
        compiler_params=pltpu.CompilerParams(
            collective_id=0, has_side_effects=True, vmem_limit_bytes=40 * 1024 * 1024),
        name="influence",
    )(
        layer_ids,
        seq_ids.reshape(1, -1),
        out_eigen,
        in_eigen,
        query_out.reshape(vectors, out_cols),
        query_in.reshape(vectors, in_cols),
        train_out.reshape(train_rows, out_all),
        train_in.reshape(train_rows, in_all),
    )


def solution(mesh):
    in_specs = (
        P("grp"),
        P(("grp", "seq")),
        P(None, "seq"),
        P(None, "seq"),
        P(None, "grp", None, "seq"),
        P(None, "grp", None, "seq"),
        P(None, ("grp", "seq"), None, None),
        P(None, ("grp", "seq"), None, None),
    )
    out_specs = P("grp", "seq")
    rows_y = max(1, PLANE_CHIPS // mesh.shape["grp"])
    return jax.shard_map(
        functools.partial(local, rows_y), mesh=mesh, in_specs=in_specs, out_specs=out_specs, check_vma=False)
```

```python
import functools

import jax
import jax.numpy as jnp
from jax import lax
from jax.experimental import pallas as pl
from jax.experimental.pallas import tpu as pltpu
from jax.sharding import PartitionSpec as P

damping = 0.1
epsilon = 1e-06

MESH = pl.DeviceIdType.MESH
CORES = 2
PLANE_CHIPS = 4
UP, DOWN, SIDE_UP, SIDE_DOWN = range(4)


def split(x):
    high = x.astype(jnp.bfloat16)
    low = (x - high.astype(jnp.float32)).astype(jnp.bfloat16)
    return jnp.concatenate([high, low], axis=0)


def both(*conditions):
    return functools.reduce(jnp.logical_and, conditions)


def kernel(depth, rows_y, layer_ref, seq_ids_ref, out_eigen_hbm, in_eigen_hbm, query_out_hbm, query_in_hbm,
           train_out_ref, train_in_ref, result_ref,
           out_eigen_ref, in_eigen_ref, query_out_ref, query_in_ref, held, train, total, load_sem, recv_sem, send_sem, core_sem, extra_sem):
    shards, chunks, vectors, width = held.shape
    queries = result_ref.shape[0]
    rank = vectors // queries
    train_rows, out_all = train_out_ref.shape
    out_chunks = chunks - 1
    grp = lax.axis_index("grp")
    me = lax.axis_index("seq")
    core = lax.rem(me, CORES)
    y = lax.rem(me // CORES, rows_y)
    z = me // (CORES * rows_y)
    balanced = rows_y == 2 and depth >= 4
    last = depth - 1

    def index(at_z, at_y, at_core):
        return (at_z * rows_y + at_y) * CORES + at_core

    loads = [
        pltpu.make_async_copy(source, target, load_sem.at[2 + place])
        for place, (source, target) in enumerate((
            (out_eigen_hbm, out_eigen_ref), (query_out_hbm, query_out_ref),
            (in_eigen_hbm, in_eigen_ref), (query_in_hbm, query_in_ref)))
    ]
    for load in loads:
        load.start()
    load_out = pltpu.make_async_copy(train_out_ref, train.at[:, pl.ds(0, out_all)], load_sem.at[0])
    load_in = pltpu.make_async_copy(train_in_ref, train.at[:, pl.ds(out_all, train_in_ref.shape[1])], load_sem.at[1])
    load_out.start()
    load_in.start()

    above, below = index(z + 1, y, core), index(z - 1, y, core)
    beside, sibling = index(z, 1 - y, core), index(z, y, 1 - core)
    has_above, has_below = z < last, z > 0

    barrier = pltpu.get_barrier_semaphore()

    def greet(other):
        pl.semaphore_signal(barrier, inc=1, device_id=(grp, other), device_id_type=MESH)

    greet(sibling)
    if rows_y == 2:
        greet(beside)
    pl.when(has_above)(lambda: greet(above))
    pl.when(has_below)(lambda: greet(below))

    def send(shard, chunk, other, sem):
        pltpu.make_async_remote_copy(
            src_ref=held.at[shard, chunk], dst_ref=held.at[shard, chunk],
            send_sem=sem, recv_sem=recv_sem.at[shard, chunk],
            device_id=(grp, other), device_id_type=MESH,
        ).start()

    def arrived(shard, chunk):
        pltpu.make_async_remote_copy(
            src_ref=held.at[shard, chunk], dst_ref=held.at[shard, chunk],
            send_sem=core_sem, recv_sem=recv_sem.at[shard, chunk],
            device_id=(grp, sibling), device_id_type=MESH,
        ).wait_recv()

    def sent(block, other, sem):
        pltpu.make_async_remote_copy(
            src_ref=block, dst_ref=block, send_sem=sem, recv_sem=recv_sem.at[0, 0],
            device_id=(grp, other), device_id_type=MESH,
        ).wait_send()

    layer = layer_ref[0]

    def damped(eigen_ref, query_ref, start):
        eigen = eigen_ref[:, start:start + width]
        stored = lax.broadcasted_iota(jnp.int32, eigen.shape, 0)
        chosen = jnp.sum(jnp.where(stored == layer, eigen, 0.0), axis=0, keepdims=True)
        return query_ref[:, start:start + width] / (chosen + damping)

    loads[0].wait()
    loads[1].wait()
    for chunk in range(out_chunks):
        held[me, chunk] = damped(out_eigen_ref, query_out_ref, chunk * width)
    loads[2].wait()
    loads[3].wait()
    held[me, out_chunks] = damped(in_eigen_ref, query_in_ref, 0)

    pl.semaphore_wait(barrier, rows_y + has_above.astype(jnp.int32) + has_below.astype(jnp.int32))

    for chunk in range(chunks):
        pl.when(has_above)(lambda: send(me, chunk, above, send_sem.at[UP, 0]))
        pl.when(has_below)(lambda: send(me, chunk, below, send_sem.at[DOWN, 0]))
        if rows_y == 2:
            send(me, chunk, beside, send_sem.at[SIDE_UP, 0])
        send(me, chunk, sibling, core_sem)

    total[...] = jnp.zeros_like(total)
    load_out.wait()
    load_in.wait()

    def absorb(shard, chunk):
        kind = chunk // out_chunks
        column = jnp.where(
            chunk < out_chunks, shard * (out_chunks * width) + chunk * width, out_all + shard * width)
        mine = split(held[shard, chunk])
        theirs = split(train[:, pl.ds(pl.multiple_of(column, width), width)])
        total[kind] += lax.dot_general(
            mine, jnp.concatenate([theirs, mine], axis=0), (((1,), (1,)), ((), ())),
            preferred_element_type=jnp.float32)

    def halved(chunk, at_core):
        return chunk < (chunks + 1) // 2 - at_core * (chunks % 2)

    def crosses(to_z, from_z, chunk, at_core):
        if not balanced:
            return True
        skip = jnp.logical_or(both(to_z == 1, from_z == 0), both(to_z == last - 1, from_z == last))
        half = jnp.logical_or(both(to_z == 0, from_z == 1), both(to_z == last, from_z == last - 1))
        return jnp.logical_not(jnp.logical_or(skip, both(half, halved(chunk, at_core))))

    def arrivals(step, chunk, at_core):
        up, down = z - step, z + step
        result = [
            (up >= 0, index(up, y, at_core), UP),
            (down <= last, index(down, y, at_core), DOWN),
        ]
        if rows_y == 2:
            up, down = z - (step - 1), z + (step - 1)
            result += [
                (both(up >= 0, crosses(z, up, chunk, at_core)), index(up, 1 - y, at_core), SIDE_UP),
                (both(step > 1, down <= last, crosses(z, down, chunk, at_core)),
                 index(down, 1 - y, at_core), SIDE_DOWN),
            ]
        if balanced:
            first = jnp.logical_or(both(z == 1, step == 2), both(z == last - 1, step == 2))
            final = both(jnp.logical_or(z == 0, z == last), step == depth, halved(chunk, at_core))
            end = jnp.where(z <= 1, 1 - z, last + last - 1 - z)
            result += [(jnp.logical_or(first, final), index(end, 1 - y, at_core), None)]
        return result

    def forward(step, chunk):
        for whether, shard, kind in arrivals(step, chunk, core):
            @pl.when(whether)
            def _():
                arrived(shard, chunk)
                if kind == UP:
                    pl.when(has_above)(lambda: send(shard, chunk, above, send_sem.at[UP, step]))
                    if rows_y == 2:
                        pl.when(crosses(z, z - step, chunk, core))(
                            lambda: send(shard, chunk, beside, send_sem.at[SIDE_UP, step]))
                if kind == DOWN:
                    pl.when(has_below)(lambda: send(shard, chunk, below, send_sem.at[DOWN, step]))
                    if rows_y == 2:
                        pl.when(crosses(z, z + step, chunk, core))(
                            lambda: send(shard, chunk, beside, send_sem.at[SIDE_DOWN, step]))
                if kind == SIDE_UP and balanced:
                    pl.when(both(step == 1, z == 0))(lambda: send(shard, chunk, above, extra_sem))
                    pl.when(both(step == 1, z == last))(lambda: send(shard, chunk, below, extra_sem))
                send(shard, chunk, sibling, core_sem)
        if balanced:
            opposite = index(z, 1 - y, core)
            late = both(step == last, halved(chunk, core))
            pl.when(both(late, z == 1))(lambda: send(opposite, chunk, below, extra_sem))
            pl.when(both(late, z == last - 1))(lambda: send(opposite, chunk, above, extra_sem))

    def absorb_all(step, chunk, at_core):
        for whether, shard, _ in arrivals(step, chunk, at_core):
            @pl.when(whether)
            def _():
                if at_core is not core:
                    arrived(shard, chunk)
                absorb(shard, chunk)

    def own(chunk, _):
        absorb(me, chunk)
        return 0

    def siblings(chunk, _):
        arrived(sibling, chunk)
        absorb(sibling, chunk)
        return 0

    lax.fori_loop(0, chunks, own, 0)

    steps = depth if rows_y == 2 else depth - 1
    other_core = 1 - core

    def tick(turn, _):
        step, chunk = turn // chunks + 1, lax.rem(turn, chunks)
        forward(step, chunk)
        absorb_all(step, chunk, core)

        @pl.when(step == 1)
        def _():
            siblings(chunk, 0)

        @pl.when(turn > 0)
        def _():
            before = turn - 1
            absorb_all(before // chunks + 1, lax.rem(before, chunks), other_core)
        return 0

    lax.fori_loop(0, steps * chunks, tick, 0)
    absorb_all(steps, chunks - 1, other_core)

    sent(held.at[pl.ds(0, shards // CORES)], sibling, core_sem)

    def left(step, _):
        pl.when(both(has_above, step <= z))(lambda: sent(held.at[0], above, send_sem.at[UP, step]))
        pl.when(both(has_below, step <= last - z))(lambda: sent(held.at[0], below, send_sem.at[DOWN, step]))
        if rows_y == 2:
            for kind, from_z, some in ((SIDE_UP, z - step, z >= step),
                                       (SIDE_DOWN, z + step, both(step > 0, z + step <= last))):
                def chunk_left(chunk, _):
                    return 0
                if not balanced:
                    pl.when(some)(lambda: sent(held.at[0], beside, send_sem.at[kind, step]))
                    continue
                skip = jnp.logical_or(both(z == 1, from_z == 0), both(z == last - 1, from_z == last))
                half = jnp.logical_or(both(z == 0, from_z == 1), both(z == last, from_z == last - 1))
                pl.when(both(some, jnp.logical_not(jnp.logical_or(skip, half))))(
                    lambda: sent(held.at[0], beside, send_sem.at[kind, step]))
                for at_core in range(CORES):
                    count = chunks // 2 + at_core * (chunks % 2)
                    pl.when(both(some, half, core == at_core))(
                        lambda: sent(held.at[0, pl.ds(0, count)], beside, send_sem.at[kind, step]))
        return 0

    lax.fori_loop(0, depth, left, 0)
    if balanced:
        for other, end, near in ((above, z == 0, z == last - 1), (below, z == last, z == 1)):
            pl.when(end)(lambda: sent(held.at[0], other, extra_sem))
            for at_core in range(CORES):
                count = (chunks + 1) // 2 - at_core * (chunks % 2)
                pl.when(both(near, core == at_core))(
                    lambda: sent(held.at[0, pl.ds(0, count)], other, extra_sem))

    def whole(kind):
        rows = total[kind, :vectors] + total[kind, vectors:]
        return (rows[:, :train_rows] + rows[:, train_rows:2 * train_rows],
                rows[:, 2 * train_rows:2 * train_rows + vectors] + rows[:, 2 * train_rows + vectors:])

    cross_out, gram_out = whole(0)
    cross_in, gram_in = whole(1)
    cross = cross_out * cross_in
    gram = gram_out * gram_in
    pool = train_rows // rank
    for query in range(queries):
        lines = slice(query * rank, (query + 1) * rank)
        norm = jnp.sum(gram[lines, lines], keepdims=True)
        scale = jnp.sqrt(norm + epsilon)
        picked = jnp.zeros(seq_ids_ref.shape, jnp.float32)
        for t in range(pool):
            unscaled = jnp.sum(cross[lines, t * rank:(t + 1) * rank], keepdims=True)
            picked += jnp.where(seq_ids_ref[...] == t, unscaled, 0.0)
        result_ref[query:query + 1, :] = picked / scale


def local(rows_y, layer_ids, seq_ids, out_eigen, in_eigen, query_out, query_in, train_out, train_in):
    shards = lax.axis_size("seq")
    _, queries, rank, out_cols = query_out.shape
    in_cols = query_in.shape[3]
    vectors = queries * rank
    train_rows = train_out.shape[1] * rank
    out_all, in_all = train_out.shape[3], train_in.shape[3]
    chunks = out_cols // in_cols + 1
    depth = shards // (CORES * rows_y)
    vmem = pl.BlockSpec(memory_space=pltpu.VMEM)
    smem = pl.BlockSpec(memory_space=pltpu.SMEM)
    hbm = pl.BlockSpec(memory_space=pltpu.HBM)
    return pl.pallas_call(
        functools.partial(kernel, depth, rows_y),
        out_shape=jax.ShapeDtypeStruct((queries, seq_ids.shape[0]), jnp.float32),
        in_specs=[smem, vmem, hbm, hbm, hbm, hbm, hbm, hbm],
        out_specs=vmem,
        scratch_shapes=[
            pltpu.VMEM(out_eigen.shape, jnp.float32),
            pltpu.VMEM(in_eigen.shape, jnp.float32),
            pltpu.VMEM((vectors, out_cols), jnp.float32),
            pltpu.VMEM((vectors, in_cols), jnp.float32),
            pltpu.VMEM((shards, chunks, vectors, in_cols), jnp.float32),
            pltpu.VMEM((train_rows, out_all + in_all), jnp.float32),
            pltpu.VMEM((2, 2 * vectors, 2 * (train_rows + vectors)), jnp.float32),
            pltpu.SemaphoreType.DMA((6,)),
            pltpu.SemaphoreType.DMA((shards, chunks)),
            pltpu.SemaphoreType.DMA((4, depth)),
            pltpu.SemaphoreType.DMA,
            pltpu.SemaphoreType.DMA,
        ],
        compiler_params=pltpu.CompilerParams(
            collective_id=0, has_side_effects=True, vmem_limit_bytes=63 * 1024 * 1024 + 896 * 1024),
        name="influence",
    )(
        layer_ids,
        seq_ids.reshape(1, -1),
        out_eigen,
        in_eigen,
        query_out.reshape(vectors, out_cols),
        query_in.reshape(vectors, in_cols),
        train_out.reshape(train_rows, out_all),
        train_in.reshape(train_rows, in_all),
    )


def solution(mesh):
    in_specs = (
        P("grp"),
        P(("grp", "seq")),
        P(None, "seq"),
        P(None, "seq"),
        P(None, "grp", None, "seq"),
        P(None, "grp", None, "seq"),
        P(None, ("grp", "seq"), None, None),
        P(None, ("grp", "seq"), None, None),
    )
    out_specs = P("grp", "seq")
    rows_y = max(1, PLANE_CHIPS // mesh.shape["grp"])
    return jax.shard_map(
        functools.partial(local, rows_y), mesh=mesh, in_specs=in_specs, out_specs=out_specs, check_vma=False)
```

```python
import functools

import jax
import jax.numpy as jnp
from jax import lax
from jax.experimental import pallas as pl
from jax.experimental.pallas import tpu as pltpu
from jax.sharding import PartitionSpec as P

damping = 0.1
epsilon = 1e-06

MESH = pl.DeviceIdType.MESH
CORES = 2
PLANE_CHIPS = 4
UP, DOWN, SIDE_UP, SIDE_DOWN = range(4)


def split(x):
    high = x.astype(jnp.bfloat16)
    low = (x - high.astype(jnp.float32)).astype(jnp.bfloat16)
    return jnp.concatenate([high, low], axis=0)


def both(*conditions):
    return functools.reduce(jnp.logical_and, conditions)


def kernel(depth, rows_y, layer_ref, seq_ids_ref, out_eigen_hbm, in_eigen_hbm, query_out_hbm, query_in_hbm,
           train_out_ref, train_in_ref, result_ref,
           out_eigen_ref, in_eigen_ref, query_out_ref, query_in_ref, held, train, total,
           guest, guest_total, given, returned,
           load_sem, recv_sem, send_sem, core_sem, extra_sem, guest_sem):
    shards, chunks, vectors, width = held.shape
    queries = result_ref.shape[0]
    rank = vectors // queries
    train_rows, out_all = train_out_ref.shape
    out_chunks = chunks - 1
    grp = lax.axis_index("grp")
    me = lax.axis_index("seq")
    core = lax.rem(me, CORES)
    y = lax.rem(me // CORES, rows_y)
    z = me // (CORES * rows_y)
    balanced = rows_y == 2 and depth >= 4
    last = depth - 1
    lent = guest.shape[1]
    along_z = lent + (chunks - lent) // 2
    at_end, near_end = jnp.logical_or(z == 0, z == last), jnp.logical_or(z == 1, z == last - 1)
    low_half = z <= 1
    partner_z = jnp.where(low_half, 1 - z, last + last - 1 - z)

    def index(at_z, at_y, at_core):
        return (at_z * rows_y + at_y) * CORES + at_core

    loads = [
        pltpu.make_async_copy(source, target, load_sem.at[2 + place])
        for place, (source, target) in enumerate((
            (out_eigen_hbm, out_eigen_ref), (query_out_hbm, query_out_ref),
            (in_eigen_hbm, in_eigen_ref), (query_in_hbm, query_in_ref)))
    ]
    for load in loads:
        load.start()
    load_out = pltpu.make_async_copy(train_out_ref, train.at[:, pl.ds(0, out_all)], load_sem.at[0])
    load_in = pltpu.make_async_copy(train_in_ref, train.at[:, pl.ds(out_all, train_in_ref.shape[1])], load_sem.at[1])
    load_out.start()
    load_in.start()

    above, below = index(z + 1, y, core), index(z - 1, y, core)
    beside, sibling = index(z, 1 - y, core), index(z, y, 1 - core)
    has_above, has_below = z < last, z > 0

    barrier = pltpu.get_barrier_semaphore()

    def greet(other):
        pl.semaphore_signal(barrier, inc=1, device_id=(grp, other), device_id_type=MESH)

    greet(sibling)
    if rows_y == 2:
        greet(beside)
    pl.when(has_above)(lambda: greet(above))
    pl.when(has_below)(lambda: greet(below))

    def send(shard, chunk, other, sem):
        pltpu.make_async_remote_copy(
            src_ref=held.at[shard, chunk], dst_ref=held.at[shard, chunk],
            send_sem=sem, recv_sem=recv_sem.at[shard, chunk],
            device_id=(grp, other), device_id_type=MESH,
        ).start()

    def arrived(shard, chunk):
        pltpu.make_async_remote_copy(
            src_ref=held.at[shard, chunk], dst_ref=held.at[shard, chunk],
            send_sem=core_sem.at[0], recv_sem=recv_sem.at[shard, chunk],
            device_id=(grp, sibling), device_id_type=MESH,
        ).wait_recv()

    def sent(block, other, sem):
        pltpu.make_async_remote_copy(
            src_ref=block, dst_ref=block, send_sem=sem, recv_sem=recv_sem.at[0, 0],
            device_id=(grp, other), device_id_type=MESH,
        ).wait_send()

    layer = layer_ref[0]

    def damped(eigen_ref, query_ref, start):
        eigen = eigen_ref[:, start:start + width]
        stored = lax.broadcasted_iota(jnp.int32, eigen.shape, 0)
        chosen = jnp.sum(jnp.where(stored == layer, eigen, 0.0), axis=0, keepdims=True)
        return query_ref[:, start:start + width] / (chosen + damping)

    loads[0].wait()
    loads[1].wait()
    for chunk in range(out_chunks):
        held[me, chunk] = damped(out_eigen_ref, query_out_ref, chunk * width)
    loads[2].wait()
    loads[3].wait()
    held[me, out_chunks] = damped(in_eigen_ref, query_in_ref, 0)

    pl.semaphore_wait(barrier, rows_y + has_above.astype(jnp.int32) + has_below.astype(jnp.int32))

    for chunk in range(chunks):
        pl.when(has_above)(lambda: send(me, chunk, above, send_sem.at[UP, 0]))
        pl.when(has_below)(lambda: send(me, chunk, below, send_sem.at[DOWN, 0]))
        if rows_y == 2:
            send(me, chunk, beside, send_sem.at[SIDE_UP, 0])
        send(me, chunk, sibling, core_sem.at[0])

    total[...] = jnp.zeros_like(total)
    if balanced:
        @pl.when(jnp.logical_not(at_end))
        def _():
            returned[...] = jnp.zeros_like(returned)

    load_out.wait()
    load_in.wait()

    def products(factors, others):
        mine, theirs = split(factors), split(others)
        return lax.dot_general(
            mine, jnp.concatenate([theirs, mine], axis=0), (((1,), (1,)), ((), ())),
            preferred_element_type=jnp.float32)

    def folded(sums):
        rows = sums[:vectors] + sums[vectors:]
        return (rows[:, :train_rows] + rows[:, train_rows:2 * train_rows],
                rows[:, 2 * train_rows:2 * train_rows + vectors] + rows[:, 2 * train_rows + vectors:])

    def absorb(shard, chunk):
        kind = chunk // out_chunks
        column = jnp.where(
            chunk < out_chunks, shard * (out_chunks * width) + chunk * width, out_all + shard * width)
        total[kind] += products(held[shard, chunk], train[:, pl.ds(pl.multiple_of(column, width), width)])

    def crosses(to_z, from_z, chunk):
        if not balanced:
            return True
        skip = jnp.logical_or(both(to_z == 1, from_z == 0), both(to_z == last - 1, from_z == last))
        part = jnp.logical_or(both(to_z == 0, from_z == 1), both(to_z == last, from_z == last - 1))
        outside = jnp.logical_or(chunk < lent, chunk >= along_z)
        return jnp.logical_not(jnp.logical_or(skip, both(part, outside)))

    def arrivals(step, chunk, at_core):
        up, down = z - step, z + step
        result = [
            (up >= 0, index(up, y, at_core), UP),
            (down <= last, index(down, y, at_core), DOWN),
        ]
        if rows_y == 2:
            up, down = z - (step - 1), z + (step - 1)
            result += [
                (both(up >= 0, crosses(z, up, chunk)), index(up, 1 - y, at_core), SIDE_UP),
                (both(step > 1, down <= last, crosses(z, down, chunk)),
                 index(down, 1 - y, at_core), SIDE_DOWN),
            ]
        if balanced:
            along = jnp.logical_or(near_end, both(at_end, chunk >= along_z))
            result += [(both(step == depth, along), index(partner_z, 1 - y, at_core), None)]
        return result

    def forward(step, chunk):
        for whether, shard, kind in arrivals(step, chunk, core):
            @pl.when(whether)
            def _():
                arrived(shard, chunk)
                if kind == UP:
                    pl.when(has_above)(lambda: send(shard, chunk, above, send_sem.at[UP, step]))
                    if rows_y == 2:
                        pl.when(crosses(z, z - step, chunk))(
                            lambda: send(shard, chunk, beside, send_sem.at[SIDE_UP, step]))
                if kind == DOWN:
                    pl.when(has_below)(lambda: send(shard, chunk, below, send_sem.at[DOWN, step]))
                    if rows_y == 2:
                        pl.when(crosses(z, z + step, chunk))(
                            lambda: send(shard, chunk, beside, send_sem.at[SIDE_DOWN, step]))
                partial = both(at_end, shard == index(partner_z, 1 - y, core)) if balanced else jnp.bool_(False)
                send(shard, chunk, sibling, core_sem.at[partial.astype(jnp.int32)])
        if balanced:
            opposite = index(z, 1 - y, core)
            for end, near, inward, outward in ((0, 1, above, below), (last, last - 1, below, above)):
                @pl.when(both(z == end, step == 1, chunk < lent))
                def _():
                    for at_core in range(CORES):
                        shard = index(near, 1 - y, at_core)
                        column = pl.multiple_of(shard * (out_chunks * width) + chunk * width, width)
                        pltpu.make_async_remote_copy(
                            src_ref=train.at[:, pl.ds(column, width)], dst_ref=guest.at[at_core, chunk],
                            send_sem=guest_sem.at[0], recv_sem=guest_sem.at[1],
                            device_id=(grp, inward), device_id_type=MESH,
                        ).start()
                pl.when(both(z == end, step == 2))(lambda: send(opposite, chunk, inward, extra_sem))

                @pl.when(both(z == near, step == last, chunk == 0))
                def _():
                    for late in range(along_z, chunks):
                        send(opposite, late, outward, extra_sem)

    def lend(sem_out, sem_in, source, target, other):
        return pltpu.make_async_remote_copy(
            src_ref=source, dst_ref=target, send_sem=guest_sem.at[sem_out], recv_sem=guest_sem.at[sem_in],
            device_id=(grp, other), device_id_type=MESH)

    def serve():
        lend(0, 1, guest, guest, sibling).wait_recv()
        guest_total[...] = jnp.zeros_like(guest_total)

        def one(place, _):
            at_core, chunk = place // lent, lax.rem(place, lent)
            guest_total[...] += products(held[index(z, 1 - y, at_core), chunk], guest[at_core, chunk])
            return 0

        lax.fori_loop(0, CORES * lent, one, 0)
        given[...] = jnp.concatenate(folded(guest_total[...]), axis=1)
        pl.when(low_half)(lambda: lend(2, 3, given, returned, below).start())
        pl.when(jnp.logical_not(low_half))(lambda: lend(2, 3, given, returned, above).start())

    def absorb_all(step, chunk, at_core):
        for whether, shard, _ in arrivals(step, chunk, at_core):
            @pl.when(whether)
            def _():
                if at_core is not core:
                    arrived(shard, chunk)
                absorb(shard, chunk)

    def own(chunk, _):
        absorb(me, chunk)
        return 0

    def siblings(chunk, _):
        arrived(sibling, chunk)
        absorb(sibling, chunk)
        return 0

    lax.fori_loop(0, chunks, own, 0)

    steps = depth if rows_y == 2 else depth - 1
    other_core = 1 - core

    def tick(turn, _):
        step, chunk = turn // chunks + 1, lax.rem(turn, chunks)
        forward(step, chunk)
        absorb_all(step, chunk, core)

        @pl.when(step == 1)
        def _():
            siblings(chunk, 0)

        @pl.when(turn > 0)
        def _():
            before = turn - 1
            absorb_all(before // chunks + 1, lax.rem(before, chunks), other_core)
        if balanced:
            pl.when(both(near_end, step == last, chunk == chunks // 2))(serve)
        return 0

    lax.fori_loop(0, steps * chunks, tick, 0)
    absorb_all(steps, chunks - 1, other_core)

    if balanced:
        pl.when(jnp.logical_not(at_end))(
            lambda: sent(held.at[pl.ds(0, shards // CORES)], sibling, core_sem.at[0]))

        @pl.when(at_end)
        def _():
            sent(held.at[pl.ds(0, shards // CORES - 1)], sibling, core_sem.at[0])
            sent(held.at[0, pl.ds(0, chunks - lent)], sibling, core_sem.at[1])
    else:
        sent(held.at[pl.ds(0, shards // CORES)], sibling, core_sem.at[0])

    def left(step, _):
        pl.when(both(has_above, step <= z))(lambda: sent(held.at[0], above, send_sem.at[UP, step]))
        pl.when(both(has_below, step <= last - z))(lambda: sent(held.at[0], below, send_sem.at[DOWN, step]))
        if rows_y == 2:
            for kind, from_z, some in ((SIDE_UP, z - step, z >= step),
                                       (SIDE_DOWN, z + step, both(step > 0, z + step <= last))):
                if not balanced:
                    pl.when(some)(lambda: sent(held.at[0], beside, send_sem.at[kind, step]))
                    continue
                skip = jnp.logical_or(both(z == 1, from_z == 0), both(z == last - 1, from_z == last))
                part = jnp.logical_or(both(z == 0, from_z == 1), both(z == last, from_z == last - 1))
                pl.when(both(some, jnp.logical_not(jnp.logical_or(skip, part))))(
                    lambda: sent(held.at[0], beside, send_sem.at[kind, step]))
                pl.when(both(some, part))(
                    lambda: sent(held.at[0, pl.ds(lent, along_z - lent)], beside, send_sem.at[kind, step]))
        return 0

    lax.fori_loop(0, depth, left, 0)
    if balanced:
        @pl.when(at_end)
        def _():
            sent(held.at[0], sibling, extra_sem)
            lend(0, 1, guest, guest, sibling).wait_send()
            lend(2, 3, returned, returned, sibling).wait_recv()

        @pl.when(near_end)
        def _():
            sent(held.at[0, pl.ds(along_z, chunks - along_z)], sibling, extra_sem)
            lend(2, 3, given, given, sibling).wait_send()

    cross_out, gram_out = folded(total[0])
    cross_in, gram_in = folded(total[1])
    if balanced:
        cross_out += returned[:, :train_rows]
        gram_out += returned[:, train_rows:]
    cross = cross_out * cross_in
    gram = gram_out * gram_in
    pool = train_rows // rank
    for query in range(queries):
        lines = slice(query * rank, (query + 1) * rank)
        norm = jnp.sum(gram[lines, lines], keepdims=True)
        scale = jnp.sqrt(norm + epsilon)
        picked = jnp.zeros(seq_ids_ref.shape, jnp.float32)
        for t in range(pool):
            unscaled = jnp.sum(cross[lines, t * rank:(t + 1) * rank], keepdims=True)
            picked += jnp.where(seq_ids_ref[...] == t, unscaled, 0.0)
        result_ref[query:query + 1, :] = picked / scale


def local(rows_y, layer_ids, seq_ids, out_eigen, in_eigen, query_out, query_in, train_out, train_in):
    shards = lax.axis_size("seq")
    _, queries, rank, out_cols = query_out.shape
    in_cols = query_in.shape[3]
    vectors = queries * rank
    train_rows = train_out.shape[1] * rank
    out_all, in_all = train_out.shape[3], train_in.shape[3]
    chunks = out_cols // in_cols + 1
    lent = min(3, chunks - 2)
    depth = shards // (CORES * rows_y)
    vmem = pl.BlockSpec(memory_space=pltpu.VMEM)
    smem = pl.BlockSpec(memory_space=pltpu.SMEM)
    hbm = pl.BlockSpec(memory_space=pltpu.HBM)
    return pl.pallas_call(
        functools.partial(kernel, depth, rows_y),
        out_shape=jax.ShapeDtypeStruct((queries, seq_ids.shape[0]), jnp.float32),
        in_specs=[smem, vmem, hbm, hbm, hbm, hbm, hbm, hbm],
        out_specs=vmem,
        scratch_shapes=[
            pltpu.VMEM(out_eigen.shape, jnp.float32),
            pltpu.VMEM(in_eigen.shape, jnp.float32),
            pltpu.VMEM((vectors, out_cols), jnp.float32),
            pltpu.VMEM((vectors, in_cols), jnp.float32),
            pltpu.VMEM((shards, chunks, vectors, in_cols), jnp.float32),
            pltpu.VMEM((train_rows, out_all + in_all), jnp.float32),
            pltpu.VMEM((2, 2 * vectors, 2 * (train_rows + vectors)), jnp.float32),
            pltpu.VMEM((CORES, lent, train_rows, in_cols), jnp.float32),
            pltpu.VMEM((2 * vectors, 2 * (train_rows + vectors)), jnp.float32),
            pltpu.VMEM((vectors, train_rows + vectors), jnp.float32),
            pltpu.VMEM((vectors, train_rows + vectors), jnp.float32),
            pltpu.SemaphoreType.DMA((6,)),
            pltpu.SemaphoreType.DMA((shards, chunks)),
            pltpu.SemaphoreType.DMA((4, depth)),
            pltpu.SemaphoreType.DMA((2,)),
            pltpu.SemaphoreType.DMA,
            pltpu.SemaphoreType.DMA((4,)),
        ],
        compiler_params=pltpu.CompilerParams(
            collective_id=0, has_side_effects=True, vmem_limit_bytes=63 * 1024 * 1024 + 896 * 1024),
        name="influence",
    )(
        layer_ids,
        seq_ids.reshape(1, -1),
        out_eigen,
        in_eigen,
        query_out.reshape(vectors, out_cols),
        query_in.reshape(vectors, in_cols),
        train_out.reshape(train_rows, out_all),
        train_in.reshape(train_rows, in_all),
    )


def solution(mesh):
    in_specs = (
        P("grp"),
        P(("grp", "seq")),
        P(None, "seq"),
        P(None, "seq"),
        P(None, "grp", None, "seq"),
        P(None, "grp", None, "seq"),
        P(None, ("grp", "seq"), None, None),
        P(None, ("grp", "seq"), None, None),
    )
    out_specs = P("grp", "seq")
    rows_y = max(1, PLANE_CHIPS // mesh.shape["grp"])
    return jax.shard_map(
        functools.partial(local, rows_y), mesh=mesh, in_specs=in_specs, out_specs=out_specs, check_vma=False)
```

```python
import functools

import jax
import jax.numpy as jnp
from jax import lax
from jax.experimental import pallas as pl
from jax.experimental.pallas import tpu as pltpu
from jax.sharding import PartitionSpec as P

damping = 0.1
epsilon = 1e-06

MESH = pl.DeviceIdType.MESH
CORES = 2
PLANE_CHIPS = 4
UP, DOWN, SIDE_UP, SIDE_DOWN = range(4)


def split(x):
    high = x.astype(jnp.bfloat16)
    low = (x - high.astype(jnp.float32)).astype(jnp.bfloat16)
    return jnp.concatenate([high, low], axis=0)


def both(*conditions):
    return functools.reduce(jnp.logical_and, conditions)


def kernel(depth, rows_y, layer_ref, seq_ids_ref, out_eigen_hbm, in_eigen_hbm, query_out_hbm, query_in_hbm,
           train_out_ref, train_in_ref, result_ref,
           out_eigen_ref, in_eigen_ref, query_out_ref, query_in_ref, held, train, total,
           guest, guest_total, given, returned,
           load_sem, recv_sem, send_sem, core_sem, extra_sem, guest_sem):
    shards, chunks, vectors, width = held.shape
    queries = result_ref.shape[0]
    rank = vectors // queries
    train_rows, out_all = train_out_ref.shape
    out_chunks = chunks - 1
    grp = lax.axis_index("grp")
    me = lax.axis_index("seq")
    core = lax.rem(me, CORES)
    y = lax.rem(me // CORES, rows_y)
    z = me // (CORES * rows_y)
    balanced = rows_y == 2 and depth >= 4
    last = depth - 1
    lent = guest.shape[1]
    along_z = lent + (chunks - lent) // 2
    at_end, near_end = jnp.logical_or(z == 0, z == last), jnp.logical_or(z == 1, z == last - 1)
    low_half = z <= 1
    partner_z = jnp.where(low_half, 1 - z, last + last - 1 - z)

    def index(at_z, at_y, at_core):
        return (at_z * rows_y + at_y) * CORES + at_core

    loads = [
        pltpu.make_async_copy(source, target, load_sem.at[2 + place])
        for place, (source, target) in enumerate((
            (out_eigen_hbm, out_eigen_ref), (query_out_hbm, query_out_ref),
            (in_eigen_hbm, in_eigen_ref), (query_in_hbm, query_in_ref)))
    ]
    for load in loads:
        load.start()
    load_out = pltpu.make_async_copy(train_out_ref, train.at[:, pl.ds(0, out_all)], load_sem.at[0])
    load_in = pltpu.make_async_copy(train_in_ref, train.at[:, pl.ds(out_all, train_in_ref.shape[1])], load_sem.at[1])

    above, below = index(z + 1, y, core), index(z - 1, y, core)
    beside, sibling = index(z, 1 - y, core), index(z, y, 1 - core)
    has_above, has_below = z < last, z > 0

    barrier = pltpu.get_barrier_semaphore()

    def greet(other):
        pl.semaphore_signal(barrier, inc=1, device_id=(grp, other), device_id_type=MESH)

    greet(sibling)
    if rows_y == 2:
        greet(beside)
    pl.when(has_above)(lambda: greet(above))
    pl.when(has_below)(lambda: greet(below))

    def send(shard, chunk, other, sem):
        pltpu.make_async_remote_copy(
            src_ref=held.at[shard, chunk], dst_ref=held.at[shard, chunk],
            send_sem=sem, recv_sem=recv_sem.at[shard, chunk],
            device_id=(grp, other), device_id_type=MESH,
        ).start()

    def arrived(shard, chunk):
        pltpu.make_async_remote_copy(
            src_ref=held.at[shard, chunk], dst_ref=held.at[shard, chunk],
            send_sem=core_sem.at[0], recv_sem=recv_sem.at[shard, chunk],
            device_id=(grp, sibling), device_id_type=MESH,
        ).wait_recv()

    def sent(block, other, sem):
        pltpu.make_async_remote_copy(
            src_ref=block, dst_ref=block, send_sem=sem, recv_sem=recv_sem.at[0, 0],
            device_id=(grp, other), device_id_type=MESH,
        ).wait_send()

    layer = layer_ref[0]

    def damped(eigen_ref, query_ref, start):
        eigen = eigen_ref[:, start:start + width]
        stored = lax.broadcasted_iota(jnp.int32, eigen.shape, 0)
        chosen = jnp.sum(jnp.where(stored == layer, eigen, 0.0), axis=0, keepdims=True)
        return query_ref[:, start:start + width] / (chosen + damping)

    for load in loads:
        load.wait()
    pl.semaphore_wait(barrier, rows_y + has_above.astype(jnp.int32) + has_below.astype(jnp.int32))

    def deferred(chunk):
        return jnp.logical_or(both(chunk >= 1, chunk < lent), chunk >= along_z)

    for chunk in range(chunks):
        if chunk < out_chunks:
            held[me, chunk] = damped(out_eigen_ref, query_out_ref, chunk * width)
        else:
            held[me, chunk] = damped(in_eigen_ref, query_in_ref, 0)
        late = balanced and (1 <= chunk < lent or chunk >= along_z)
        pl.when(both(has_above, z != last - 1) if late else has_above)(
            lambda: send(me, chunk, above, send_sem.at[UP, 0]))
        pl.when(both(has_below, z != 1) if late else has_below)(
            lambda: send(me, chunk, below, send_sem.at[DOWN, 0]))
        if rows_y == 2:
            send(me, chunk, beside, send_sem.at[SIDE_UP, 0])
        send(me, chunk, sibling, core_sem.at[0])

    load_out.start()
    load_in.start()

    total[...] = jnp.zeros_like(total)
    if balanced:
        @pl.when(jnp.logical_not(at_end))
        def _():
            returned[...] = jnp.zeros_like(returned)

    load_out.wait()
    load_in.wait()

    def products(factors, others):
        mine, theirs = split(factors), split(others)
        return lax.dot_general(
            mine, jnp.concatenate([theirs, mine], axis=0), (((1,), (1,)), ((), ())),
            preferred_element_type=jnp.float32)

    def folded(sums):
        rows = sums[:vectors] + sums[vectors:]
        return (rows[:, :train_rows] + rows[:, train_rows:2 * train_rows],
                rows[:, 2 * train_rows:2 * train_rows + vectors] + rows[:, 2 * train_rows + vectors:])

    def absorb(shard, chunk):
        kind = chunk // out_chunks
        column = jnp.where(
            chunk < out_chunks, shard * (out_chunks * width) + chunk * width, out_all + shard * width)
        total[kind] += products(held[shard, chunk], train[:, pl.ds(pl.multiple_of(column, width), width)])

    def crosses(to_z, from_z, chunk):
        if not balanced:
            return True
        skip = jnp.logical_or(both(to_z == 1, from_z == 0), both(to_z == last - 1, from_z == last))
        part = jnp.logical_or(both(to_z == 0, from_z == 1), both(to_z == last, from_z == last - 1))
        outside = jnp.logical_or(chunk < lent, chunk >= along_z)
        return jnp.logical_not(jnp.logical_or(skip, both(part, outside)))

    def arrivals(step, chunk, at_core):
        up, down = z - step, z + step
        prompt = True
        if balanced:
            prompt = jnp.logical_not(both(at_end, step == 1, deferred(chunk)))
        result = [
            (both(up >= 0, prompt), index(up, y, at_core), UP),
            (both(down <= last, prompt), index(down, y, at_core), DOWN),
        ]
        if rows_y == 2:
            up, down = z - (step - 1), z + (step - 1)
            result += [
                (both(up >= 0, crosses(z, up, chunk)), index(up, 1 - y, at_core), SIDE_UP),
                (both(step > 1, down <= last, crosses(z, down, chunk)),
                 index(down, 1 - y, at_core), SIDE_DOWN),
            ]
        if balanced:
            along = jnp.logical_or(near_end, both(at_end, chunk >= along_z))
            result += [(both(step == depth, at_end, deferred(chunk)), index(partner_z, y, at_core), None)]
            result += [(both(step == depth, along), index(partner_z, 1 - y, at_core), None)]
        return result

    def forward(step, chunk):
        for whether, shard, kind in arrivals(step, chunk, core):
            @pl.when(whether)
            def _():
                arrived(shard, chunk)
                if kind == UP:
                    pl.when(has_above)(lambda: send(shard, chunk, above, send_sem.at[UP, step]))
                    if rows_y == 2:
                        pl.when(crosses(z, z - step, chunk))(
                            lambda: send(shard, chunk, beside, send_sem.at[SIDE_UP, step]))
                if kind == DOWN:
                    pl.when(has_below)(lambda: send(shard, chunk, below, send_sem.at[DOWN, step]))
                    if rows_y == 2:
                        pl.when(crosses(z, z + step, chunk))(
                            lambda: send(shard, chunk, beside, send_sem.at[SIDE_DOWN, step]))
                partial = both(at_end, shard == index(partner_z, 1 - y, core)) if balanced else jnp.bool_(False)
                send(shard, chunk, sibling, core_sem.at[partial.astype(jnp.int32)])
        if balanced:
            opposite = index(z, 1 - y, core)
            for end, near, inward, outward in ((0, 1, above, below), (last, last - 1, below, above)):
                @pl.when(both(z == end, step == 1, chunk < lent))
                def _():
                    for at_core in range(CORES):
                        shard = index(near, 1 - y, at_core)
                        column = pl.multiple_of(shard * (out_chunks * width) + chunk * width, width)
                        pltpu.make_async_remote_copy(
                            src_ref=train.at[:, pl.ds(column, width)], dst_ref=guest.at[at_core, chunk],
                            send_sem=guest_sem.at[0], recv_sem=guest_sem.at[1],
                            device_id=(grp, inward), device_id_type=MESH,
                        ).start()
                pl.when(both(z == end, step == 2))(lambda: send(opposite, chunk, inward, extra_sem))

                @pl.when(both(z == near, step == last - 1, chunk == chunks - 1))
                def _():
                    kind = DOWN if end == 0 else UP
                    for late in list(range(1, lent)) + list(range(along_z, chunks)):
                        send(me, late, outward, send_sem.at[kind, 0])
                    for late in range(along_z, chunks):
                        send(opposite, late, outward, extra_sem)

    def lend(sem_out, sem_in, source, target, other):
        return pltpu.make_async_remote_copy(
            src_ref=source, dst_ref=target, send_sem=guest_sem.at[sem_out], recv_sem=guest_sem.at[sem_in],
            device_id=(grp, other), device_id_type=MESH)

    def serve():
        lend(0, 1, guest, guest, sibling).wait_recv()
        guest_total[...] = jnp.zeros_like(guest_total)

        def one(place, _):
            at_core, chunk = place // lent, lax.rem(place, lent)
            guest_total[...] += products(held[index(z, 1 - y, at_core), chunk], guest[at_core, chunk])
            return 0

        lax.fori_loop(0, CORES * lent, one, 0)
        given[...] = jnp.concatenate(folded(guest_total[...]), axis=1)
        pl.when(low_half)(lambda: lend(2, 3, given, returned, below).start())
        pl.when(jnp.logical_not(low_half))(lambda: lend(2, 3, given, returned, above).start())

    def absorb_all(step, chunk, at_core):
        for whether, shard, _ in arrivals(step, chunk, at_core):
            @pl.when(whether)
            def _():
                if at_core is not core:
                    arrived(shard, chunk)
                absorb(shard, chunk)

    def own(chunk, _):
        absorb(me, chunk)
        return 0

    def siblings(chunk, _):
        arrived(sibling, chunk)
        absorb(sibling, chunk)
        return 0

    lax.fori_loop(0, chunks, own, 0)

    steps = depth if rows_y == 2 else depth - 1
    other_core = 1 - core

    def tick(turn, _):
        step, chunk = turn // chunks + 1, lax.rem(turn, chunks)
        forward(step, chunk)
        absorb_all(step, chunk, core)

        @pl.when(step == 1)
        def _():
            siblings(chunk, 0)

        @pl.when(turn > 0)
        def _():
            before = turn - 1
            absorb_all(before // chunks + 1, lax.rem(before, chunks), other_core)
        if balanced:
            pl.when(both(near_end, step == last, chunk == chunks // 2))(serve)
        return 0

    lax.fori_loop(0, steps * chunks, tick, 0)
    absorb_all(steps, chunks - 1, other_core)

    if balanced:
        pl.when(jnp.logical_not(at_end))(
            lambda: sent(held.at[pl.ds(0, shards // CORES)], sibling, core_sem.at[0]))

        @pl.when(at_end)
        def _():
            sent(held.at[pl.ds(0, shards // CORES - 1)], sibling, core_sem.at[0])
            sent(held.at[0, pl.ds(0, chunks - lent)], sibling, core_sem.at[1])
    else:
        sent(held.at[pl.ds(0, shards // CORES)], sibling, core_sem.at[0])

    def left(step, _):
        pl.when(both(has_above, step <= z))(lambda: sent(held.at[0], above, send_sem.at[UP, step]))
        pl.when(both(has_below, step <= last - z))(lambda: sent(held.at[0], below, send_sem.at[DOWN, step]))
        if rows_y == 2:
            for kind, from_z, some in ((SIDE_UP, z - step, z >= step),
                                       (SIDE_DOWN, z + step, both(step > 0, z + step <= last))):
                if not balanced:
                    pl.when(some)(lambda: sent(held.at[0], beside, send_sem.at[kind, step]))
                    continue
                skip = jnp.logical_or(both(z == 1, from_z == 0), both(z == last - 1, from_z == last))
                part = jnp.logical_or(both(z == 0, from_z == 1), both(z == last, from_z == last - 1))
                pl.when(both(some, jnp.logical_not(jnp.logical_or(skip, part))))(
                    lambda: sent(held.at[0], beside, send_sem.at[kind, step]))
                pl.when(both(some, part))(
                    lambda: sent(held.at[0, pl.ds(lent, along_z - lent)], beside, send_sem.at[kind, step]))
        return 0

    lax.fori_loop(0, depth, left, 0)
    if balanced:
        @pl.when(at_end)
        def _():
            sent(held.at[0], sibling, extra_sem)
            lend(0, 1, guest, guest, sibling).wait_send()
            lend(2, 3, returned, returned, sibling).wait_recv()

        @pl.when(near_end)
        def _():
            sent(held.at[0, pl.ds(along_z, chunks - along_z)], sibling, extra_sem)
            lend(2, 3, given, given, sibling).wait_send()

    cross_out, gram_out = folded(total[0])
    cross_in, gram_in = folded(total[1])
    if balanced:
        cross_out += returned[:, :train_rows]
        gram_out += returned[:, train_rows:]
    cross = cross_out * cross_in
    gram = gram_out * gram_in
    pool = train_rows // rank
    for query in range(queries):
        lines = slice(query * rank, (query + 1) * rank)
        norm = jnp.sum(gram[lines, lines], keepdims=True)
        scale = jnp.sqrt(norm + epsilon)
        picked = jnp.zeros(seq_ids_ref.shape, jnp.float32)
        for t in range(pool):
            unscaled = jnp.sum(cross[lines, t * rank:(t + 1) * rank], keepdims=True)
            picked += jnp.where(seq_ids_ref[...] == t, unscaled, 0.0)
        result_ref[query:query + 1, :] = picked / scale


def local(rows_y, layer_ids, seq_ids, out_eigen, in_eigen, query_out, query_in, train_out, train_in):
    shards = lax.axis_size("seq")
    _, queries, rank, out_cols = query_out.shape
    in_cols = query_in.shape[3]
    vectors = queries * rank
    train_rows = train_out.shape[1] * rank
    out_all, in_all = train_out.shape[3], train_in.shape[3]
    chunks = out_cols // in_cols + 1
    lent = min(3, chunks - 2)
    depth = shards // (CORES * rows_y)
    vmem = pl.BlockSpec(memory_space=pltpu.VMEM)
    smem = pl.BlockSpec(memory_space=pltpu.SMEM)
    hbm = pl.BlockSpec(memory_space=pltpu.HBM)
    return pl.pallas_call(
        functools.partial(kernel, depth, rows_y),
        out_shape=jax.ShapeDtypeStruct((queries, seq_ids.shape[0]), jnp.float32),
        in_specs=[smem, vmem, hbm, hbm, hbm, hbm, hbm, hbm],
        out_specs=vmem,
        scratch_shapes=[
            pltpu.VMEM(out_eigen.shape, jnp.float32),
            pltpu.VMEM(in_eigen.shape, jnp.float32),
            pltpu.VMEM((vectors, out_cols), jnp.float32),
            pltpu.VMEM((vectors, in_cols), jnp.float32),
            pltpu.VMEM((shards, chunks, vectors, in_cols), jnp.float32),
            pltpu.VMEM((train_rows, out_all + in_all), jnp.float32),
            pltpu.VMEM((2, 2 * vectors, 2 * (train_rows + vectors)), jnp.float32),
            pltpu.VMEM((CORES, lent, train_rows, in_cols), jnp.float32),
            pltpu.VMEM((2 * vectors, 2 * (train_rows + vectors)), jnp.float32),
            pltpu.VMEM((vectors, train_rows + vectors), jnp.float32),
            pltpu.VMEM((vectors, train_rows + vectors), jnp.float32),
            pltpu.SemaphoreType.DMA((6,)),
            pltpu.SemaphoreType.DMA((shards, chunks)),
            pltpu.SemaphoreType.DMA((4, depth)),
            pltpu.SemaphoreType.DMA((2,)),
            pltpu.SemaphoreType.DMA,
            pltpu.SemaphoreType.DMA((4,)),
        ],
        compiler_params=pltpu.CompilerParams(
            collective_id=0, has_side_effects=True, vmem_limit_bytes=64 * 1024 * 1024),
        name="influence",
    )(
        layer_ids,
        seq_ids.reshape(1, -1),
        out_eigen,
        in_eigen,
        query_out.reshape(vectors, out_cols),
        query_in.reshape(vectors, in_cols),
        train_out.reshape(train_rows, out_all),
        train_in.reshape(train_rows, in_all),
    )


def solution(mesh):
    in_specs = (
        P("grp"),
        P(("grp", "seq")),
        P(None, "seq"),
        P(None, "seq"),
        P(None, "grp", None, "seq"),
        P(None, "grp", None, "seq"),
        P(None, ("grp", "seq"), None, None),
        P(None, ("grp", "seq"), None, None),
    )
    out_specs = P("grp", "seq")
    rows_y = max(1, PLANE_CHIPS // mesh.shape["grp"])
    return jax.shard_map(
        functools.partial(local, rows_y), mesh=mesh, in_specs=in_specs, out_specs=out_specs, check_vma=False)
```

```python
import functools

import jax
import jax.numpy as jnp
from jax import lax
from jax.experimental import pallas as pl
from jax.experimental.pallas import tpu as pltpu
from jax.sharding import PartitionSpec as P

damping = 0.1
epsilon = 1e-06

MESH = pl.DeviceIdType.MESH
CORES = 2
PLANE_CHIPS = 4
UP, DOWN, SIDE_UP, SIDE_DOWN = range(4)


def split(x):
    high = x.astype(jnp.bfloat16)
    low = (x - high.astype(jnp.float32)).astype(jnp.bfloat16)
    return jnp.concatenate([high, low], axis=0)


def both(*conditions):
    return functools.reduce(jnp.logical_and, conditions)


def kernel(depth, rows_y, layer_hbm, seq_ids_hbm, out_eigen_hbm, in_eigen_hbm, query_out_hbm, query_in_hbm,
           train_out_ref, train_in_ref, result_ref,
           layer_ref, seq_ids_ref, out_eigen_ref, in_eigen_ref, query_out_ref, query_in_ref, held, train, total,
           guest, guest_total, given, returned,
           load_sem, recv_sem, send_sem, core_sem, extra_sem, guest_sem):
    shards, chunks, vectors, width = held.shape
    queries = result_ref.shape[0]
    rank = vectors // queries
    train_rows, out_all = train_out_ref.shape
    out_chunks = chunks - 1
    grp = lax.axis_index("grp")
    me = lax.axis_index("seq")
    core = lax.rem(me, CORES)
    y = lax.rem(me // CORES, rows_y)
    z = me // (CORES * rows_y)
    balanced = rows_y == 2 and depth >= 4
    last = depth - 1
    lent = guest.shape[1]
    along_z = lent + (chunks - lent) // 2
    at_end, near_end = jnp.logical_or(z == 0, z == last), jnp.logical_or(z == 1, z == last - 1)
    low_half = z <= 1
    partner_z = jnp.where(low_half, 1 - z, last + last - 1 - z)

    def index(at_z, at_y, at_core):
        return (at_z * rows_y + at_y) * CORES + at_core

    load_out = pltpu.make_async_copy(train_out_ref, train.at[:, pl.ds(0, out_all)], load_sem.at[0])
    load_in = pltpu.make_async_copy(train_in_ref, train.at[:, pl.ds(out_all, train_in_ref.shape[1])], load_sem.at[1])

    above, below = index(z + 1, y, core), index(z - 1, y, core)
    beside, sibling = index(z, 1 - y, core), index(z, y, 1 - core)
    has_above, has_below = z < last, z > 0

    barrier = pltpu.get_barrier_semaphore()

    def greet(other):
        pl.semaphore_signal(barrier, inc=1, device_id=(grp, other), device_id_type=MESH)

    greet(sibling)
    if rows_y == 2:
        greet(beside)
    pl.when(has_above)(lambda: greet(above))
    pl.when(has_below)(lambda: greet(below))

    loads = [
        pltpu.make_async_copy(source, target, load_sem.at[2 + place])
        for place, (source, target) in enumerate((
            (out_eigen_hbm, out_eigen_ref), (query_out_hbm, query_out_ref),
            (in_eigen_hbm, in_eigen_ref), (query_in_hbm, query_in_ref),
            (layer_hbm, layer_ref), (seq_ids_hbm, seq_ids_ref)))
    ]
    for load in loads:
        load.start()

    def send(shard, chunk, other, sem):
        pltpu.make_async_remote_copy(
            src_ref=held.at[shard, chunk], dst_ref=held.at[shard, chunk],
            send_sem=sem, recv_sem=recv_sem.at[shard, chunk],
            device_id=(grp, other), device_id_type=MESH,
        ).start()

    def arrived(shard, chunk):
        pltpu.make_async_remote_copy(
            src_ref=held.at[shard, chunk], dst_ref=held.at[shard, chunk],
            send_sem=core_sem.at[0], recv_sem=recv_sem.at[shard, chunk],
            device_id=(grp, sibling), device_id_type=MESH,
        ).wait_recv()

    def sent(block, other, sem):
        pltpu.make_async_remote_copy(
            src_ref=block, dst_ref=block, send_sem=sem, recv_sem=recv_sem.at[0, 0],
            device_id=(grp, other), device_id_type=MESH,
        ).wait_send()


    def damped(eigen_ref, query_ref, start):
        eigen = eigen_ref[:, start:start + width]
        stored = lax.broadcasted_iota(jnp.int32, eigen.shape, 0)
        chosen = jnp.sum(jnp.where(stored == layer_ref[...], eigen, 0.0), axis=0, keepdims=True)
        return query_ref[:, start:start + width] / (chosen + damping)

    for load in loads:
        load.wait()
    pl.semaphore_wait(barrier, rows_y + has_above.astype(jnp.int32) + has_below.astype(jnp.int32))

    def deferred(chunk):
        return jnp.logical_or(both(chunk >= 1, chunk < lent), chunk >= along_z)

    for chunk in range(chunks):
        if chunk < out_chunks:
            held[me, chunk] = damped(out_eigen_ref, query_out_ref, chunk * width)
        else:
            held[me, chunk] = damped(in_eigen_ref, query_in_ref, 0)
        late = balanced and (1 <= chunk < lent or chunk >= along_z)
        pl.when(both(has_above, z != last - 1) if late else has_above)(
            lambda: send(me, chunk, above, send_sem.at[UP, 0]))
        pl.when(both(has_below, z != 1) if late else has_below)(
            lambda: send(me, chunk, below, send_sem.at[DOWN, 0]))
        if rows_y == 2:
            send(me, chunk, beside, send_sem.at[SIDE_UP, 0])
        send(me, chunk, sibling, core_sem.at[0])

    load_out.start()
    load_in.start()

    total[...] = jnp.zeros_like(total)
    if balanced:
        @pl.when(jnp.logical_not(at_end))
        def _():
            returned[...] = jnp.zeros_like(returned)

    load_out.wait()
    load_in.wait()

    def products(factors, others):
        mine, theirs = split(factors), split(others)
        return lax.dot_general(
            mine, jnp.concatenate([theirs, mine], axis=0), (((1,), (1,)), ((), ())),
            preferred_element_type=jnp.float32)

    def folded(sums):
        rows = sums[:vectors] + sums[vectors:]
        return (rows[:, :train_rows] + rows[:, train_rows:2 * train_rows],
                rows[:, 2 * train_rows:2 * train_rows + vectors] + rows[:, 2 * train_rows + vectors:])

    def absorb(shard, chunk):
        kind = chunk // out_chunks
        column = jnp.where(
            chunk < out_chunks, shard * (out_chunks * width) + chunk * width, out_all + shard * width)
        total[kind] += products(held[shard, chunk], train[:, pl.ds(pl.multiple_of(column, width), width)])

    def crosses(to_z, from_z, chunk):
        if not balanced:
            return True
        skip = jnp.logical_or(both(to_z == 1, from_z == 0), both(to_z == last - 1, from_z == last))
        part = jnp.logical_or(both(to_z == 0, from_z == 1), both(to_z == last, from_z == last - 1))
        outside = jnp.logical_or(chunk < lent, chunk >= along_z)
        return jnp.logical_not(jnp.logical_or(skip, both(part, outside)))

    def arrivals(step, chunk, at_core):
        up, down = z - step, z + step
        prompt = True
        if balanced:
            prompt = jnp.logical_not(both(at_end, step == 1, deferred(chunk)))
        result = [
            (both(up >= 0, prompt), index(up, y, at_core), UP),
            (both(down <= last, prompt), index(down, y, at_core), DOWN),
        ]
        if rows_y == 2:
            up, down = z - (step - 1), z + (step - 1)
            result += [
                (both(up >= 0, crosses(z, up, chunk)), index(up, 1 - y, at_core), SIDE_UP),
                (both(step > 1, down <= last, crosses(z, down, chunk)),
                 index(down, 1 - y, at_core), SIDE_DOWN),
            ]
        if balanced:
            along = jnp.logical_or(near_end, both(at_end, chunk >= along_z))
            result += [(both(step == depth, at_end, deferred(chunk)), index(partner_z, y, at_core), None)]
            result += [(both(step == depth, along), index(partner_z, 1 - y, at_core), None)]
        return result

    def forward(step, chunk):
        for whether, shard, kind in arrivals(step, chunk, core):
            @pl.when(whether)
            def _():
                arrived(shard, chunk)
                if kind == UP:
                    pl.when(has_above)(lambda: send(shard, chunk, above, send_sem.at[UP, step]))
                    if rows_y == 2:
                        pl.when(crosses(z, z - step, chunk))(
                            lambda: send(shard, chunk, beside, send_sem.at[SIDE_UP, step]))
                if kind == DOWN:
                    pl.when(has_below)(lambda: send(shard, chunk, below, send_sem.at[DOWN, step]))
                    if rows_y == 2:
                        pl.when(crosses(z, z + step, chunk))(
                            lambda: send(shard, chunk, beside, send_sem.at[SIDE_DOWN, step]))
                partial = both(at_end, shard == index(partner_z, 1 - y, core)) if balanced else jnp.bool_(False)
                send(shard, chunk, sibling, core_sem.at[partial.astype(jnp.int32)])
        if balanced:
            opposite = index(z, 1 - y, core)
            for end, near, inward, outward in ((0, 1, above, below), (last, last - 1, below, above)):
                @pl.when(both(z == end, step == 1, chunk < lent))
                def _():
                    for at_core in range(CORES):
                        shard = index(near, 1 - y, at_core)
                        column = pl.multiple_of(shard * (out_chunks * width) + chunk * width, width)
                        pltpu.make_async_remote_copy(
                            src_ref=train.at[:, pl.ds(column, width)], dst_ref=guest.at[at_core, chunk],
                            send_sem=guest_sem.at[0], recv_sem=guest_sem.at[1],
                            device_id=(grp, inward), device_id_type=MESH,
                        ).start()
                pl.when(both(z == end, step == 2))(lambda: send(opposite, chunk, inward, extra_sem))

                @pl.when(both(z == near, step == last - 1, chunk == chunks - 1))
                def _():
                    kind = DOWN if end == 0 else UP
                    for late in list(range(1, lent)) + list(range(along_z, chunks)):
                        send(me, late, outward, send_sem.at[kind, 0])
                    for late in range(along_z, chunks):
                        send(opposite, late, outward, extra_sem)

    def lend(sem_out, sem_in, source, target, other):
        return pltpu.make_async_remote_copy(
            src_ref=source, dst_ref=target, send_sem=guest_sem.at[sem_out], recv_sem=guest_sem.at[sem_in],
            device_id=(grp, other), device_id_type=MESH)

    def serve():
        lend(0, 1, guest, guest, sibling).wait_recv()
        guest_total[...] = jnp.zeros_like(guest_total)

        def one(place, _):
            at_core, chunk = place // lent, lax.rem(place, lent)
            guest_total[...] += products(held[index(z, 1 - y, at_core), chunk], guest[at_core, chunk])
            return 0

        lax.fori_loop(0, CORES * lent, one, 0)
        given[...] = jnp.concatenate(folded(guest_total[...]), axis=1)
        pl.when(low_half)(lambda: lend(2, 3, given, returned, below).start())
        pl.when(jnp.logical_not(low_half))(lambda: lend(2, 3, given, returned, above).start())

    def absorb_all(step, chunk, at_core):
        for whether, shard, _ in arrivals(step, chunk, at_core):
            @pl.when(whether)
            def _():
                if at_core is not core:
                    arrived(shard, chunk)
                absorb(shard, chunk)

    def own(chunk, _):
        absorb(me, chunk)
        return 0

    def siblings(chunk, _):
        arrived(sibling, chunk)
        absorb(sibling, chunk)
        return 0

    lax.fori_loop(0, chunks, own, 0)

    steps = depth if rows_y == 2 else depth - 1
    other_core = 1 - core

    def tick(turn, _):
        step, chunk = turn // chunks + 1, lax.rem(turn, chunks)
        before = turn - 1

        early = both(step == steps, at_end)

        def absorb_before():
            absorb_all(before // chunks + 1, lax.rem(before, chunks), other_core)

        pl.when(both(turn > 0, early))(absorb_before)
        forward(step, chunk)
        absorb_all(step, chunk, core)

        @pl.when(step == 1)
        def _():
            siblings(chunk, 0)

        pl.when(both(turn > 0, jnp.logical_not(early)))(absorb_before)
        if balanced:
            pl.when(both(near_end, step == last, chunk == chunks // 2))(serve)
        return 0

    lax.fori_loop(0, steps * chunks, tick, 0)
    absorb_all(steps, chunks - 1, other_core)

    if balanced:
        pl.when(jnp.logical_not(at_end))(
            lambda: sent(held.at[pl.ds(0, shards // CORES)], sibling, core_sem.at[0]))

        @pl.when(at_end)
        def _():
            sent(held.at[pl.ds(0, shards // CORES - 1)], sibling, core_sem.at[0])
            sent(held.at[0, pl.ds(0, chunks - lent)], sibling, core_sem.at[1])
    else:
        sent(held.at[pl.ds(0, shards // CORES)], sibling, core_sem.at[0])

    def left(step, _):
        pl.when(both(has_above, step <= z))(lambda: sent(held.at[0], above, send_sem.at[UP, step]))
        pl.when(both(has_below, step <= last - z))(lambda: sent(held.at[0], below, send_sem.at[DOWN, step]))
        if rows_y == 2:
            for kind, from_z, some in ((SIDE_UP, z - step, z >= step),
                                       (SIDE_DOWN, z + step, both(step > 0, z + step <= last))):
                if not balanced:
                    pl.when(some)(lambda: sent(held.at[0], beside, send_sem.at[kind, step]))
                    continue
                skip = jnp.logical_or(both(z == 1, from_z == 0), both(z == last - 1, from_z == last))
                part = jnp.logical_or(both(z == 0, from_z == 1), both(z == last, from_z == last - 1))
                pl.when(both(some, jnp.logical_not(jnp.logical_or(skip, part))))(
                    lambda: sent(held.at[0], beside, send_sem.at[kind, step]))
                pl.when(both(some, part))(
                    lambda: sent(held.at[0, pl.ds(lent, along_z - lent)], beside, send_sem.at[kind, step]))
        return 0

    lax.fori_loop(0, depth, left, 0)
    if balanced:
        @pl.when(at_end)
        def _():
            sent(held.at[0], sibling, extra_sem)
            lend(0, 1, guest, guest, sibling).wait_send()
            lend(2, 3, returned, returned, sibling).wait_recv()

        @pl.when(near_end)
        def _():
            sent(held.at[0, pl.ds(along_z, chunks - along_z)], sibling, extra_sem)
            lend(2, 3, given, given, sibling).wait_send()

    cross_out, gram_out = folded(total[0])
    cross_in, gram_in = folded(total[1])
    if balanced:
        cross_out += returned[:, :train_rows]
        gram_out += returned[:, train_rows:]
    cross = cross_out * cross_in
    gram = gram_out * gram_in
    pool = train_rows // rank
    for query in range(queries):
        lines = slice(query * rank, (query + 1) * rank)
        norm = jnp.sum(gram[lines, lines], keepdims=True)
        scale = jnp.sqrt(norm + epsilon)
        picked = jnp.zeros(seq_ids_ref.shape, jnp.float32)
        for t in range(pool):
            unscaled = jnp.sum(cross[lines, t * rank:(t + 1) * rank], keepdims=True)
            picked += jnp.where(seq_ids_ref[...] == t, unscaled, 0.0)
        result_ref[query:query + 1, :] = picked / scale


def local(rows_y, layer_ids, seq_ids, out_eigen, in_eigen, query_out, query_in, train_out, train_in):
    shards = lax.axis_size("seq")
    _, queries, rank, out_cols = query_out.shape
    in_cols = query_in.shape[3]
    vectors = queries * rank
    train_rows = train_out.shape[1] * rank
    out_all, in_all = train_out.shape[3], train_in.shape[3]
    chunks = out_cols // in_cols + 1
    lent = min(3, chunks - 2)
    depth = shards // (CORES * rows_y)
    vmem = pl.BlockSpec(memory_space=pltpu.VMEM)
    hbm = pl.BlockSpec(memory_space=pltpu.HBM)
    return pl.pallas_call(
        functools.partial(kernel, depth, rows_y),
        out_shape=jax.ShapeDtypeStruct((queries, seq_ids.shape[0]), jnp.float32),
        in_specs=[hbm] * 8,
        out_specs=vmem,
        scratch_shapes=[
            pltpu.VMEM((1, 1), jnp.int32),
            pltpu.VMEM((1, seq_ids.shape[0]), jnp.int32),
            pltpu.VMEM(out_eigen.shape, jnp.float32),
            pltpu.VMEM(in_eigen.shape, jnp.float32),
            pltpu.VMEM((vectors, out_cols), jnp.float32),
            pltpu.VMEM((vectors, in_cols), jnp.float32),
            pltpu.VMEM((shards, chunks, vectors, in_cols), jnp.float32),
            pltpu.VMEM((train_rows, out_all + in_all), jnp.float32),
            pltpu.VMEM((2, 2 * vectors, 2 * (train_rows + vectors)), jnp.float32),
            pltpu.VMEM((CORES, lent, train_rows, in_cols), jnp.float32),
            pltpu.VMEM((2 * vectors, 2 * (train_rows + vectors)), jnp.float32),
            pltpu.VMEM((vectors, train_rows + vectors), jnp.float32),
            pltpu.VMEM((vectors, train_rows + vectors), jnp.float32),
            pltpu.SemaphoreType.DMA((8,)),
            pltpu.SemaphoreType.DMA((shards, chunks)),
            pltpu.SemaphoreType.DMA((4, depth)),
            pltpu.SemaphoreType.DMA((2,)),
            pltpu.SemaphoreType.DMA,
            pltpu.SemaphoreType.DMA((4,)),
        ],
        compiler_params=pltpu.CompilerParams(
            collective_id=0, has_side_effects=True, vmem_limit_bytes=64 * 1024 * 1024),
        name="influence",
    )(
        layer_ids.reshape(1, 1),
        seq_ids.reshape(1, -1),
        out_eigen,
        in_eigen,
        query_out.reshape(vectors, out_cols),
        query_in.reshape(vectors, in_cols),
        train_out.reshape(train_rows, out_all),
        train_in.reshape(train_rows, in_all),
    )


def solution(mesh):
    in_specs = (
        P("grp"),
        P(("grp", "seq")),
        P(None, "seq"),
        P(None, "seq"),
        P(None, "grp", None, "seq"),
        P(None, "grp", None, "seq"),
        P(None, ("grp", "seq"), None, None),
        P(None, ("grp", "seq"), None, None),
    )
    out_specs = P("grp", "seq")
    rows_y = max(1, PLANE_CHIPS // mesh.shape["grp"])
    return jax.shard_map(
        functools.partial(local, rows_y), mesh=mesh, in_specs=in_specs, out_specs=out_specs, check_vma=False)
```
